32 devices in a mesh: row: 4 (over y, core), col: 8 (over z, x).
Axes of the slice: x: 2, y: 2, z: 4, core: 2. Of those that a mesh axis runs over, the one named last changes fastest.
Arguments:
- features: float32 [4096, 1536], P('row', 'col'), may hold values from -6 to 6
Outputs:
- panel: float32 [4096, 512], P('row')
- trailing: float32 [4096, 4096], P('row', 'col')
The draws below stay inside these ranges and needn't reach their ends.
All inputs are finite; a program needn't handle non-finite values.
Results may differ from the reference program's by a relative error of at most 0.0003.
Values sent between devices are 32-bit elements; how exact they have to be, the bound alone decides.
A program may use at most 64 MiB of HBM per device.

```python
import jax
import jax.numpy as jnp
from jax import lax

D = 1536
PANEL = 512
ORDER = 4096


def level_of(own_key, extent, cuts, smallest, high):
    gain = 1.0
    for axis_at, parts in cuts:
        draws = jax.random.uniform(jax.random.fold_in(jax.random.fold_in(own_key, 6), axis_at), (parts,), jnp.float32, smallest / len(cuts), high / len(cuts))
        gain = gain * jnp.repeat(jnp.exp(draws), extent[axis_at] // parts).reshape((-1,) + (1,) * (len(extent) - 1 - axis_at))
    return gain


def bell_draw(key, extent, width, reach, split=(), held_as=jnp.bfloat16):
    result = width * jax.random.normal(key, extent, jnp.float32)
    if split:
        result = result * level_of(key, extent, split, -0.22, 0.18)
    return jnp.clip(result, -reach, reach).astype(held_as)


def setup_inputs(seed: int = 0) -> dict:
    key_of = jax.random.split(jax.random.key(seed), 2)
    return {
        "features": bell_draw(key_of[0], (ORDER, D), 1.0, 6.0, ((0, 4), (1, 8)), jnp.float32),
    }


gamma_scale = 0.6
ridge_value = 0.05

def gauss_tile(left_rows, right_rows, row_start, col_start):
    left_sq = jnp.sum(left_rows * left_rows, axis=1)
    right_sq = jnp.sum(right_rows * right_rows, axis=1)
    inner_prod = jnp.dot(left_rows.astype(jnp.float32), right_rows.T.astype(jnp.float32), precision=lax.Precision.HIGHEST, preferred_element_type=jnp.float32)
    distance = left_sq[:, None] + right_sq[None, :] - 2.0 * inner_prod
    kernel_value = jnp.exp(-distance * (gamma_scale / D))
    row_index = row_start + jnp.arange(left_rows.shape[0], dtype=jnp.int32)
    col_index = col_start + jnp.arange(right_rows.shape[0], dtype=jnp.int32)
    return kernel_value + jnp.where(row_index[:, None] == col_index[None, :], ridge_value, 0.0).astype(jnp.float32)

def reference(features):
    blocks = features.shape[0] // PANEL
    head_rows = features[:PANEL]
    corner = gauss_tile(head_rows, head_rows, 0, 0)
    chol_factor = jnp.linalg.cholesky(corner)
    inverse = lax.linalg.triangular_solve(chol_factor, jnp.eye(PANEL, dtype=jnp.float32), left_side=True, lower=True)
    starts = (jnp.arange(blocks, dtype=jnp.int32) * PANEL).astype(jnp.int32)

    def panel_block(block_start):
        block_rows = lax.dynamic_slice_in_dim(features, block_start, PANEL, 0)
        side_tile = gauss_tile(block_rows, head_rows, block_start, 0)
        return jnp.dot(side_tile.astype(jnp.float32), inverse.T.astype(jnp.float32), precision=lax.Precision.HIGHEST, preferred_element_type=jnp.float32)
    solved = lax.map(panel_block, starts).reshape(features.shape[0], PANEL)
    panel_out = jnp.concatenate([chol_factor, solved[PANEL:]], axis=0)
    masked = jnp.concatenate([jnp.zeros((PANEL, PANEL), jnp.float32), solved[PANEL:]], axis=0)

    def trailing_block(block_start):
        block_rows = lax.dynamic_slice_in_dim(features, block_start, PANEL, 0)
        kernel_tile = gauss_tile(block_rows, features, block_start, 0)
        block_panel = lax.dynamic_slice_in_dim(masked, block_start, PANEL, 0)
        return kernel_tile - jnp.dot(block_panel.astype(jnp.float32), masked.T.astype(jnp.float32), precision=lax.Precision.HIGHEST, preferred_element_type=jnp.float32)
    trailing = lax.map(trailing_block, starts).reshape(features.shape[0], features.shape[0])
    return (panel_out, trailing)
```

```python
import functools

import jax
import jax.numpy as jnp
from jax import lax
from jax.experimental import pallas as pl
from jax.experimental.pallas import tpu as pltpu
from jax.sharding import PartitionSpec as P

D = 1536


gamma_scale = 0.6
ridge_value = 0.05

LANES = 128
GROUP = 8


def spread(value, axis, source):
    kept = jnp.where(lax.axis_index(axis) == source, value, 0).astype(value.dtype)
    return lax.psum(kept, axis)


def gauss_tile(left_rows, right_rows, row_start, col_start, precision=lax.Precision.HIGH):
    left_sq = jnp.sum(left_rows * left_rows, axis=1)
    right_sq = jnp.sum(right_rows * right_rows, axis=1)
    inner_prod = jnp.dot(
        left_rows, right_rows.T, precision=precision, preferred_element_type=jnp.float32
    )
    distance = left_sq[:, None] + right_sq[None, :] - 2.0 * inner_prod
    kernel_value = jnp.exp(-distance * (gamma_scale / D))
    row_index = row_start + jnp.arange(left_rows.shape[0], dtype=jnp.int32)
    col_index = col_start + jnp.arange(right_rows.shape[0], dtype=jnp.int32)
    return kernel_value + jnp.where(
        row_index[:, None] == col_index[None, :], ridge_value, 0.0
    ).astype(jnp.float32)


def solve_rows(some_rows, head_rows, first_index, inverse):
    side_tile = gauss_tile(some_rows, head_rows, first_index, 0)
    return jnp.dot(
        side_tile, inverse.T, precision=lax.Precision.HIGH, preferred_element_type=jnp.float32
    )


def split_three(value):
    high = value.astype(jnp.bfloat16).astype(jnp.float32)
    rest = value - high
    middle = rest.astype(jnp.bfloat16).astype(jnp.float32)
    return high, middle, rest - middle


def outer_update(rows_here):
    high, middle, low = split_three(rows_here)
    right = jnp.concatenate([high, middle, high, low, high, middle], axis=0).astype(jnp.bfloat16)
    left = jnp.concatenate(
        [part[:, :LANES] for part in (high, high, middle, high, low, middle)], axis=0
    ).astype(jnp.bfloat16)
    return lax.dot_general(
        left, right, (((0,), (0,)), ((), ())), preferred_element_type=jnp.float32
    )


def factor_group(block_ref, done_ref, first):
    left_rows = [block_ref[pl.ds(first + t, 1), pl.ds(0, LANES)] for t in range(GROUP)]
    right_rows = [block_ref[pl.ds(first + t, 1), pl.ds(LANES, LANES)] for t in range(GROUP)]
    entry = {}
    for i in range(GROUP):
        for t in range(i + 1):
            entry[i, t] = jnp.broadcast_to(
                left_rows[i][:, first + t : first + t + 1], (1, LANES)
            )
    for t in range(GROUP):
        scale = lax.rsqrt(entry[t, t])
        ratio = [None] * GROUP
        for i in range(t + 1, GROUP):
            ratio[i] = entry[i, t] * scale
        for i in range(t + 1, GROUP):
            for k in range(t + 1, i + 1):
                entry[i, k] = entry[i, k] - ratio[i] * ratio[k]
        left_rows[t] = left_rows[t] * scale
        right_rows[t] = right_rows[t] * scale
        for i in range(t + 1, GROUP):
            left_rows[i] = left_rows[i] - ratio[i] * left_rows[t]
            right_rows[i] = right_rows[i] - ratio[i] * right_rows[t]
    for t in range(GROUP):
        done_ref[pl.ds(first + t, 1), pl.ds(0, LANES)] = left_rows[t]
        done_ref[pl.ds(first + t, 1), pl.ds(LANES, LANES)] = right_rows[t]
    after = first + GROUP
    if after < LANES:
        change = outer_update(done_ref[pl.ds(first, GROUP), :])
        block_ref[pl.ds(after, LANES - after), :] -= change[after:, :]


def factor_kernel(corner_ref, chol_ref, inverse_ref, work, block, done):
    size = corner_ref.shape[0]
    work[:, pl.ds(0, size)] = corner_ref[...]
    work[:, pl.ds(size, size)] = (
        lax.broadcasted_iota(jnp.int32, (size, size), 0)
        == lax.broadcasted_iota(jnp.int32, (size, size), 1)
    ).astype(jnp.float32)

    def step(at, carry):
        start = pl.multiple_of(at * LANES, LANES)
        rows = pl.ds(start, LANES)
        block[:, pl.ds(0, LANES)] = work[rows, rows]
        block[:, pl.ds(LANES, LANES)] = (
            lax.broadcasted_iota(jnp.int32, (LANES, LANES), 0)
            == lax.broadcasted_iota(jnp.int32, (LANES, LANES), 1)
        ).astype(jnp.float32)
        for first in range(0, LANES, GROUP):
            factor_group(block, done, first)
        solved = jnp.dot(
            done[:, pl.ds(LANES, LANES)],
            work[rows, :],
            precision=lax.Precision.HIGHEST,
            preferred_element_type=jnp.float32,
        )
        upper = solved[:, :size]
        keep = (
            start + lax.broadcasted_iota(jnp.int32, (LANES, size), 0)
            <= lax.broadcasted_iota(jnp.int32, (LANES, size), 1)
        )
        chol_ref[:, rows] = jnp.where(keep, upper, 0.0).T
        inverse_ref[rows, :] = solved[:, size:]
        for other in range(LANES, size, LANES):

            @pl.when(other > start)
            def _(other=other):
                across = chol_ref[pl.ds(other, LANES), rows]
                work[pl.ds(other, LANES), :] -= jnp.dot(
                    across,
                    solved,
                    precision=lax.Precision.HIGHEST,
                    preferred_element_type=jnp.float32,
                )

        return carry

    lax.fori_loop(0, size // LANES, step, 0)


def factor(corner):
    size = corner.shape[0]
    return pl.pallas_call(
        factor_kernel,
        out_shape=[jax.ShapeDtypeStruct((size, size), jnp.float32)] * 2,
        in_specs=[pl.BlockSpec(memory_space=pltpu.VMEM)],
        out_specs=[pl.BlockSpec(memory_space=pltpu.VMEM)] * 2,
        scratch_shapes=[
            pltpu.VMEM((size, 2 * size), jnp.float32),
            pltpu.VMEM((LANES, 2 * LANES), jnp.float32),
            pltpu.VMEM((LANES, 2 * LANES), jnp.float32),
        ],
        compiler_params=pltpu.CompilerParams(vmem_limit_bytes=32 * 1024 * 1024),
        name="factor",
        cost_estimate=pl.CostEstimate(
            flops=size * size * size * 4, bytes_accessed=3 * 4 * size * size, transcendentals=size
        ),
    )(corner)


def on_device(features):
    row_count = lax.axis_size("row")
    col_count = lax.axis_size("col")
    row_id = lax.axis_index("row")
    col_id = lax.axis_index("col")
    row_feat = lax.all_gather(features, "col", axis=1, tiled=True)
    row_height = row_feat.shape[0]
    col_ratio = col_count // row_count
    panel_width = row_height // col_ratio
    row_offset = col_id % col_ratio * panel_width
    owner_row = col_id // col_ratio
    col_feat = spread(
        lax.dynamic_slice_in_dim(row_feat, row_offset, panel_width, 0), "row", owner_row
    )
    head_part = spread(features[:panel_width], "row", 0)
    head_rows = lax.all_gather(head_part, "col", axis=1, tiled=True)
    corner = gauss_tile(head_rows, head_rows, 0, 0, lax.Precision.HIGHEST)
    chol_factor, inverse = factor(corner)
    row_start = row_id * row_height
    col_start = col_id * panel_width
    kernel_tile = gauss_tile(row_feat, col_feat, row_start, col_start)
    row_piece = row_height // col_count
    piece_rows = lax.dynamic_slice_in_dim(row_feat, col_id * row_piece, row_piece, 0)
    piece_solved = solve_rows(piece_rows, head_rows, row_start + col_id * row_piece, inverse)
    solved_rows = lax.all_gather(piece_solved, "col", axis=0, tiled=True)
    positions = row_start + jnp.arange(row_height, dtype=jnp.int32)
    top_rows = jnp.concatenate(
        [chol_factor, jnp.zeros((row_height - panel_width, panel_width), jnp.float32)], axis=0
    )
    panel_out = jnp.where(positions[:, None] < panel_width, top_rows, solved_rows)
    masked = jnp.where(positions[:, None] < panel_width, 0.0, solved_rows)
    far_panel = solve_rows(col_feat, head_rows, col_start, inverse)
    col_positions = col_start + jnp.arange(panel_width, dtype=jnp.int32)
    far_panel = jnp.where(col_positions[:, None] < panel_width, 0.0, far_panel)
    trailing = kernel_tile - jnp.dot(
        masked, far_panel.T, precision=lax.Precision.HIGH, preferred_element_type=jnp.float32
    )
    return (panel_out, trailing)


def solution(mesh):
    return jax.shard_map(
        on_device,
        mesh=mesh,
        in_specs=(P("row", "col"),),
        out_specs=(P("row", None), P("row", "col")),
        check_vma=False,
    )
```

```python
import functools

import jax
import jax.numpy as jnp
from jax import lax
from jax.experimental import pallas as pl
from jax.experimental.pallas import tpu as pltpu
from jax.sharding import PartitionSpec as P

D = 1536


gamma_scale = 0.6
ridge_value = 0.05

MESH = pl.DeviceIdType.MESH
LANES = 128
GROUP = 8


def square_sums(turned):
    return jnp.sum(turned * turned, axis=0)


def gauss_tile(left, right, row_start, col_start, precision=lax.Precision.HIGH):
    inner_prod = lax.dot_general(
        left,
        right,
        (((0,), (0,)), ((), ())),
        precision=precision,
        preferred_element_type=jnp.float32,
    )
    distance = square_sums(left)[:, None] + square_sums(right)[None, :] - 2.0 * inner_prod
    kernel_value = jnp.exp(-distance * (gamma_scale / D))
    row_index = row_start + jnp.arange(left.shape[1], dtype=jnp.int32)
    col_index = col_start + jnp.arange(right.shape[1], dtype=jnp.int32)
    return kernel_value + jnp.where(
        row_index[:, None] == col_index[None, :], ridge_value, 0.0
    ).astype(jnp.float32)


def split_three(value):
    high = value.astype(jnp.bfloat16).astype(jnp.float32)
    rest = value - high
    middle = rest.astype(jnp.bfloat16).astype(jnp.float32)
    return high, middle, rest - middle


def outer_update(rows_here):
    high, middle, low = split_three(rows_here)
    right = jnp.concatenate([high, middle, high, low, high, middle], axis=0).astype(jnp.bfloat16)
    left = jnp.concatenate(
        [part[:, :LANES] for part in (high, high, middle, high, low, middle)], axis=0
    ).astype(jnp.bfloat16)
    return lax.dot_general(
        left, right, (((0,), (0,)), ((), ())), preferred_element_type=jnp.float32
    )


def factor_group(block_ref, done_ref, first):
    left_rows = [block_ref[pl.ds(first + t, 1), pl.ds(0, LANES)] for t in range(GROUP)]
    right_rows = [block_ref[pl.ds(first + t, 1), pl.ds(LANES, LANES)] for t in range(GROUP)]
    entry = {}
    for i in range(GROUP):
        for t in range(i + 1):
            entry[i, t] = jnp.broadcast_to(
                left_rows[i][:, first + t : first + t + 1], (1, LANES)
            )
    for t in range(GROUP):
        scale = lax.rsqrt(entry[t, t])
        scale = scale * (1.5 - 0.5 * entry[t, t] * scale * scale)
        ratio = [None] * GROUP
        for i in range(t + 1, GROUP):
            ratio[i] = entry[i, t] * scale
        for i in range(t + 1, GROUP):
            for k in range(t + 1, i + 1):
                entry[i, k] = entry[i, k] - ratio[i] * ratio[k]
        left_rows[t] = left_rows[t] * scale
        right_rows[t] = right_rows[t] * scale
        for i in range(t + 1, GROUP):
            left_rows[i] = left_rows[i] - ratio[i] * left_rows[t]
            right_rows[i] = right_rows[i] - ratio[i] * right_rows[t]
    for t in range(GROUP):
        done_ref[pl.ds(first + t, 1), pl.ds(0, LANES)] = left_rows[t]
        done_ref[pl.ds(first + t, 1), pl.ds(LANES, LANES)] = right_rows[t]
    after = first + GROUP
    if after < LANES:
        change = outer_update(done_ref[pl.ds(first, GROUP), :])
        block_ref[pl.ds(after, LANES - after), :] -= change[after:, :]


def factor_kernel(corner_ref, chol_ref, inverse_ref, work, block, done):
    size = corner_ref.shape[0]
    work[:, pl.ds(0, size)] = corner_ref[...]
    work[:, pl.ds(size, size)] = (
        lax.broadcasted_iota(jnp.int32, (size, size), 0)
        == lax.broadcasted_iota(jnp.int32, (size, size), 1)
    ).astype(jnp.float32)

    def step(at, carry):
        start = pl.multiple_of(at * LANES, LANES)
        rows = pl.ds(start, LANES)
        block[:, pl.ds(0, LANES)] = work[rows, rows]
        block[:, pl.ds(LANES, LANES)] = (
            lax.broadcasted_iota(jnp.int32, (LANES, LANES), 0)
            == lax.broadcasted_iota(jnp.int32, (LANES, LANES), 1)
        ).astype(jnp.float32)
        for first in range(0, LANES, GROUP):
            factor_group(block, done, first)
        solved = jnp.dot(
            done[:, pl.ds(LANES, LANES)],
            work[rows, :],
            precision=lax.Precision.HIGHEST,
            preferred_element_type=jnp.float32,
        )
        upper = solved[:, :size]
        keep = (
            start + lax.broadcasted_iota(jnp.int32, (LANES, size), 0)
            <= lax.broadcasted_iota(jnp.int32, (LANES, size), 1)
        )
        chol_ref[:, rows] = jnp.where(keep, upper, 0.0).T
        inverse_ref[rows, :] = solved[:, size:]
        for other in range(LANES, size, LANES):

            @pl.when(other > start)
            def _(other=other):
                across = chol_ref[pl.ds(other, LANES), rows]
                work[pl.ds(other, LANES), :] -= jnp.dot(
                    across,
                    solved,
                    precision=lax.Precision.HIGHEST,
                    preferred_element_type=jnp.float32,
                )

        return carry

    lax.fori_loop(0, size // LANES, step, 0)


def factor(corner):
    size = corner.shape[0]
    return pl.pallas_call(
        factor_kernel,
        out_shape=[jax.ShapeDtypeStruct((size, size), jnp.float32)] * 2,
        in_specs=[pl.BlockSpec(memory_space=pltpu.VMEM)],
        out_specs=[pl.BlockSpec(memory_space=pltpu.VMEM)] * 2,
        scratch_shapes=[
            pltpu.VMEM((size, 2 * size), jnp.float32),
            pltpu.VMEM((LANES, 2 * LANES), jnp.float32),
            pltpu.VMEM((LANES, 2 * LANES), jnp.float32),
        ],
        compiler_params=pltpu.CompilerParams(vmem_limit_bytes=32 * 1024 * 1024),
        name="factor",
        cost_estimate=pl.CostEstimate(
            flops=size * size * size * 4, bytes_accessed=3 * 4 * size * size, transcendentals=size
        ),
    )(corner)


def gather_kernel(row_count, col_count, own_ref, row_out, head_out, col_out, own_sem, row_sem, head_sem, col_sem,
                  up_sem, down_sem, side_sem, head_send, col_up, col_down, local_sem):
    halves, width, _ = own_ref.shape
    row = lax.axis_index("row")
    col = lax.axis_index("col")
    lines = col_count // 2
    line, side = col // 2, col % 2
    owner = col // halves
    part = col % halves
    started = []

    def where(cond, act):
        pl.when(cond)(act)

    def send(cond, source, target, send_sem, recv_sem, to_row, to_col):
        copy = pltpu.make_async_remote_copy(
            src_ref=source,
            dst_ref=target,
            send_sem=send_sem,
            recv_sem=recv_sem,
            device_id=(to_row, to_col),
            device_id_type=MESH,
        )
        where(cond, copy.start)
        started.append((cond, copy.wait_send))

    def keep(cond, source, target, sem):
        copy = pltpu.make_async_copy(source, target, sem)
        where(cond, copy.start)
        started.append((cond, copy.wait))

    def arrived(cond, target, recv_sem):
        copy = pltpu.make_async_remote_copy(
            src_ref=target,
            dst_ref=target,
            send_sem=recv_sem,
            recv_sem=recv_sem,
            device_id=(row, col),
            device_id_type=MESH,
        )
        where(cond, copy.wait_recv)

    def slot(half, chunk):
        return row_out.at[half, pl.ds(pl.multiple_of(chunk * width, 8), width), :]

    def piece(ref, chunk):
        return ref.at[pl.ds(pl.multiple_of(chunk * width, 8), width), :]

    neighbours = (
        (line < lines - 1, row, col + 2),
        (line > 0, row, col - 2),
        (row >= 0, row, line * 2 + 1 - side),
        (row < row_count - 1, row + 1, col),
        (row > 0, row - 1, col),
    )
    barrier = pltpu.get_barrier_semaphore()
    for cond, to_row, to_col in neighbours:
        where(
            cond,
            lambda to_row=to_row, to_col=to_col: pl.semaphore_signal(
                barrier, inc=1, device_id=(to_row, to_col), device_id_type=MESH
            ),
        )
    pl.semaphore_wait(barrier, sum(cond.astype(jnp.int32) for cond, _, _ in neighbours))

    def go_up(half, chunk, source, cond):
        send(cond & (line < lines - 1), source, slot(half, chunk), up_sem.at[half, chunk],
             row_sem.at[half, chunk], row, col + 2)

    def go_down(half, chunk, source, cond):
        send(cond & (line > 0), source, slot(half, chunk), down_sem.at[half, chunk],
             row_sem.at[half, chunk], row, col - 2)

    def go_side(half, chunk, source, cond):
        send(cond, source, slot(half, chunk), side_sem.at[half, chunk],
             row_sem.at[half, chunk], row, line * 2 + 1 - side)

    def pass_on(half, chunk, source, cond):
        if half == 0:
            first = cond & (row == 0)
            send(first, source, piece(head_out, chunk), head_send.at[chunk], head_sem.at[chunk], row + 1, col)
            keep(first, source, piece(head_out, chunk), local_sem.at[0, chunk])
        mine = cond & (row == owner) & (part == half)
        send(mine & (row < row_count - 1), source, piece(col_out, chunk), col_up.at[chunk],
             col_sem.at[chunk], row + 1, col)
        send(mine & (row > 0), source, piece(col_out, chunk), col_down.at[chunk],
             col_sem.at[chunk], row - 1, col)
        keep(mine, source, piece(col_out, chunk), local_sem.at[1, chunk])

    always = row >= 0
    for half in range(halves):
        own = own_ref.at[half]
        go_up(half, col, own, always)
        go_down(half, col, own, always)
        go_side(half, col, own, always)
        pass_on(half, col, own, always)
        keep(always, own, slot(half, col), own_sem.at[half])

    def orders():
        for away in range(lines):
            if away == 0:
                yield away, line, always
            else:
                yield away, line - away, line >= away
                yield -away, line + away, line + away < lines

    for half in range(halves):
        for away, at, cond in orders():
            at = jnp.clip(at, 0, lines - 1)
            chunk = at * 2 + side
            if away != 0:
                arrived(cond, slot(half, chunk), row_sem.at[half, chunk])
                (go_up if away > 0 else go_down)(half, chunk, slot(half, chunk), cond)
                go_side(half, chunk, slot(half, chunk), cond)
                pass_on(half, chunk, slot(half, chunk), cond)
            chunk = at * 2 + 1 - side
            arrived(cond, slot(half, chunk), row_sem.at[half, chunk])
            pass_on(half, chunk, slot(half, chunk), cond)
        if half == 0:
            for away, at, cond in orders():
                at = jnp.clip(at, 0, lines - 1)
                for chunk in (at * 2 + side, at * 2 + 1 - side):
                    taken = cond & (row > 0)
                    arrived(taken, piece(head_out, chunk), head_sem.at[chunk])
                    send(taken & (row < row_count - 1), piece(head_out, chunk), piece(head_out, chunk),
                         head_send.at[chunk], head_sem.at[chunk], row + 1, col)
    for away, at, cond in orders():
        at = jnp.clip(at, 0, lines - 1)
        for chunk in (at * 2 + side, at * 2 + 1 - side):
            arrived(cond & (row != owner), piece(col_out, chunk), col_sem.at[chunk])
            send(cond & (row > owner) & (row < row_count - 1), piece(col_out, chunk), piece(col_out, chunk),
                 col_up.at[chunk], col_sem.at[chunk], row + 1, col)
            send(cond & (row < owner) & (row > 0), piece(col_out, chunk), piece(col_out, chunk),
                 col_down.at[chunk], col_sem.at[chunk], row - 1, col)
    for cond, wait in started:
        where(cond, wait)


def gather_all(turned, row_count, col_count):
    halves, width, centers = turned.shape
    depth = width * col_count
    dma = pltpu.SemaphoreType.DMA
    return pl.pallas_call(
        functools.partial(gather_kernel, row_count, col_count),
        out_shape=[
            jax.ShapeDtypeStruct((halves, depth, centers), jnp.float32),
            jax.ShapeDtypeStruct((depth, centers), jnp.float32),
            jax.ShapeDtypeStruct((depth, centers), jnp.float32),
        ],
        in_specs=[pl.BlockSpec(memory_space=pl.ANY)],
        out_specs=[pl.BlockSpec(memory_space=pl.ANY)] * 3,
        scratch_shapes=[
            dma((halves,)),
            dma((halves, col_count)),
            dma((col_count,)),
            dma((col_count,)),
            dma((halves, col_count)),
            dma((halves, col_count)),
            dma((halves, col_count)),
            dma((col_count,)),
            dma((col_count,)),
            dma((col_count,)),
            dma((2, col_count)),
        ],
        compiler_params=pltpu.CompilerParams(collective_id=0, has_side_effects=True),
        name="gather",
    )(turned)


def on_device(features):
    row_count = lax.axis_size("row")
    col_count = lax.axis_size("col")
    row_id = lax.axis_index("row")
    col_id = lax.axis_index("col")
    row_height, width = features.shape
    halves = col_count // row_count
    panel_width = row_height // halves
    turned = features.reshape(halves, panel_width, width).transpose(0, 2, 1)
    row_parts, head, column = gather_all(turned, row_count, col_count)
    corner = gauss_tile(head, head, 0, 0, lax.Precision.HIGHEST)
    chol_factor, inverse = factor(corner)
    row_start = row_id * row_height
    col_start = col_id * panel_width

    def solve(some, first):
        return lax.dot_general(
            gauss_tile(some, head, first, 0),
            inverse,
            (((1,), (1,)), ((), ())),
            precision=lax.Precision.HIGH,
            preferred_element_type=jnp.float32,
        )

    far_panel = jnp.where(col_id == 0, 0.0, solve(column, col_start))
    panels, trails = [], []
    for part in range(halves):
        first = row_start + part * panel_width
        solved = solve(row_parts[part], first)
        top = first == 0
        panels.append(jnp.where(top, chol_factor, solved))
        masked = jnp.where(top, 0.0, solved)
        trails.append(
            gauss_tile(row_parts[part], column, first, col_start)
            - lax.dot_general(
                masked,
                far_panel,
                (((1,), (1,)), ((), ())),
                precision=lax.Precision.HIGH,
                preferred_element_type=jnp.float32,
            )
        )
    return (jnp.concatenate(panels, axis=0), jnp.concatenate(trails, axis=0))


def solution(mesh):
    return jax.shard_map(
        on_device,
        mesh=mesh,
        in_specs=(P("row", "col"),),
        out_specs=(P("row", None), P("row", "col")),
        check_vma=False,
    )
```

```python
import functools

import jax
import jax.numpy as jnp
from jax import lax
from jax.experimental import pallas as pl
from jax.experimental.pallas import tpu as pltpu
from jax.sharding import PartitionSpec as P

D = 1536


gamma_scale = 0.6
ridge_value = 0.05

MESH = pl.DeviceIdType.MESH
LANES = 128
GROUP = 8


def split_three(value):
    high = value.astype(jnp.bfloat16).astype(jnp.float32)
    rest = value - high
    middle = rest.astype(jnp.bfloat16).astype(jnp.float32)
    return high, middle, rest - middle


def outer_update(rows_here):
    high, middle, low = split_three(rows_here)
    right = jnp.concatenate([high, middle, high, low, high, middle], axis=0).astype(jnp.bfloat16)
    left = jnp.concatenate(
        [part[:, :LANES] for part in (high, high, middle, high, low, middle)], axis=0
    ).astype(jnp.bfloat16)
    return lax.dot_general(
        left, right, (((0,), (0,)), ((), ())), preferred_element_type=jnp.float32
    )


def factor_group(block_ref, done_ref, first):
    left_rows = [block_ref[pl.ds(first + t, 1), pl.ds(0, LANES)] for t in range(GROUP)]
    right_rows = [block_ref[pl.ds(first + t, 1), pl.ds(LANES, LANES)] for t in range(GROUP)]
    entry = {}
    for i in range(GROUP):
        for t in range(i + 1):
            entry[i, t] = jnp.broadcast_to(
                left_rows[i][:, first + t : first + t + 1], (1, LANES)
            )
    for t in range(GROUP):
        scale = lax.rsqrt(entry[t, t])
        scale = scale * (1.5 - 0.5 * entry[t, t] * scale * scale)
        ratio = [None] * GROUP
        for i in range(t + 1, GROUP):
            ratio[i] = entry[i, t] * scale
        for i in range(t + 1, GROUP):
            for k in range(t + 1, i + 1):
                entry[i, k] = entry[i, k] - ratio[i] * ratio[k]
        left_rows[t] = left_rows[t] * scale
        right_rows[t] = right_rows[t] * scale
        for i in range(t + 1, GROUP):
            left_rows[i] = left_rows[i] - ratio[i] * left_rows[t]
            right_rows[i] = right_rows[i] - ratio[i] * right_rows[t]
    for t in range(GROUP):
        done_ref[pl.ds(first + t, 1), pl.ds(0, LANES)] = left_rows[t]
        done_ref[pl.ds(first + t, 1), pl.ds(LANES, LANES)] = right_rows[t]
    after = first + GROUP
    if after < LANES:
        change = outer_update(done_ref[pl.ds(first, GROUP), :])
        block_ref[pl.ds(after, LANES - after), :] -= change[after:, :]


def stacked(value, order, axis):
    parts = split_three(value)
    return jnp.concatenate([parts[at].astype(jnp.bfloat16) for at in order], axis=axis)


FINE = ((0, 0, 1, 0, 2, 1), (0, 1, 0, 2, 0, 1))
PLAIN = ((0, 0, 1), (0, 1, 0))


def product(left, right, axis, orders):
    return lax.dot_general(
        stacked(left, orders[0], axis),
        stacked(right, orders[1], axis),
        (((axis,), (axis,)), ((), ())),
        preferred_element_type=jnp.float32,
    )


def diagonal(rows, columns, offset):
    return (
        offset + lax.broadcasted_iota(jnp.int32, (rows, columns), 0)
        == lax.broadcasted_iota(jnp.int32, (rows, columns), 1)
    )


def gauss_into(out_ref, left, right, offset, orders, step):
    depth, rows = left.shape
    columns = right.shape[1]
    out_ref[...] = jnp.zeros((rows, columns), jnp.float32)

    def add(at, squares):
        span = pl.ds(pl.multiple_of(at * step, step), step)
        one, two = left[span, :], right[span, :]
        out_ref[...] += product(one, two, 0, orders)
        return (
            squares[0] + jnp.sum(one * one, axis=0, keepdims=True),
            squares[1] + jnp.sum(two * two, axis=0, keepdims=True),
        )

    left_sq, right_sq = lax.fori_loop(
        0,
        depth // step,
        add,
        (jnp.zeros((1, rows), jnp.float32), jnp.zeros((1, columns), jnp.float32)),
    )
    left_sq = jnp.broadcast_to(left_sq, (LANES, rows)).T[:, :1]
    distance = left_sq + right_sq - 2.0 * out_ref[...]
    kernel_value = jnp.exp(-distance * (gamma_scale / D))
    out_ref[...] = kernel_value + jnp.where(
        diagonal(rows, columns, offset), ridge_value, 0.0
    )


def factor_into(corner_ref, chol_ref, inverse_ref, work, block, done, beside):
    size = corner_ref.shape[0]
    work[:, pl.ds(0, size)] = corner_ref[...]
    work[:, pl.ds(size, size)] = diagonal(size, size, 0).astype(jnp.float32)

    def step(at, carry):
        start = pl.multiple_of(at * LANES, LANES)
        rows = pl.ds(start, LANES)
        block[:, pl.ds(0, LANES)] = work[rows, rows]
        block[:, pl.ds(LANES, LANES)] = diagonal(LANES, LANES, 0).astype(jnp.float32)
        for first in range(0, LANES, GROUP):
            factor_group(block, done, first)
        solved = jnp.dot(
            done[:, pl.ds(LANES, LANES)],
            work[rows, :],
            precision=lax.Precision.HIGHEST,
            preferred_element_type=jnp.float32,
        )
        upper = solved[:, :size]
        keep = (
            start + lax.broadcasted_iota(jnp.int32, (LANES, size), 0)
            <= lax.broadcasted_iota(jnp.int32, (LANES, size), 1)
        )
        chol_ref[:, rows] = jnp.where(keep, upper, 0.0).T
        inverse_ref[rows, :] = solved[:, size:]
        for other in range(LANES, size, LANES):

            @pl.when(other > start)
            def _(other=other):
                across = chol_ref[pl.ds(other, LANES), rows]
                work[pl.ds(other, LANES), :] -= jnp.dot(
                    across,
                    solved,
                    precision=lax.Precision.HIGHEST,
                    preferred_element_type=jnp.float32,
                )

        beside(at)
        return carry

    lax.fori_loop(0, size // LANES, step, 0)


def panel_kernel(row_count, col_count, own_ref, panel_ref, trail_ref, rows_ref, head_ref, column_ref,
                 corner, chol, inverse, far, side_tile, tile, work, block, done,
                 row_sem, head_sem, col_sem, up_sem, down_sem, side_sem, head_send, col_up, col_down):
    halves, width, centers = own_ref.shape
    row = lax.axis_index("row")
    col = lax.axis_index("col")
    lines = col_count // 2
    line, side = col // 2, col % 2
    owner = col // halves
    part = col % halves

    def copy_of(source, target, send_sem, recv_sem, to_row, to_col):
        return pltpu.make_async_remote_copy(
            src_ref=source,
            dst_ref=target,
            send_sem=send_sem,
            recv_sem=recv_sem,
            device_id=(to_row, to_col),
            device_id_type=MESH,
        )

    def arrived(cond, target, recv_sem):
        pl.when(cond)(lambda: copy_of(target, target, recv_sem, recv_sem, row, col).wait_recv())

    def send(cond, source, target, send_sem, recv_sem, to_row, to_col):
        pl.when(cond)(lambda: copy_of(source, target, send_sem, recv_sem, to_row, to_col).start())

    def slot(half, chunk):
        return rows_ref.at[half, pl.ds(pl.multiple_of(chunk * width, 8), width), :]

    def piece(ref, chunk):
        return ref.at[pl.ds(pl.multiple_of(chunk * width, 8), width), :]

    neighbours = (
        (line < lines - 1, row, col + 2),
        (line > 0, row, col - 2),
        (row >= 0, row, line * 2 + 1 - side),
        (row < row_count - 1, row + 1, col),
        (row > 0, row - 1, col),
    )
    barrier = pltpu.get_barrier_semaphore()
    for cond, to_row, to_col in neighbours:
        pl.when(cond)(
            lambda to_row=to_row, to_col=to_col: pl.semaphore_signal(
                barrier, inc=1, device_id=(to_row, to_col), device_id_type=MESH
            )
        )
    pl.semaphore_wait(barrier, sum(cond.astype(jnp.int32) for cond, _, _ in neighbours))

    def go_up(half, chunk, source, cond):
        send(cond & (line < lines - 1), source, slot(half, chunk), up_sem.at[half, chunk],
             row_sem.at[half, chunk], row, col + 2)

    def go_down(half, chunk, source, cond):
        send(cond & (line > 0), source, slot(half, chunk), down_sem.at[half, chunk],
             row_sem.at[half, chunk], row, col - 2)

    def go_side(half, chunk, source, cond):
        send(cond, source, slot(half, chunk), side_sem.at[half, chunk],
             row_sem.at[half, chunk], row, line * 2 + 1 - side)

    def pass_on(half, chunk, source, cond):
        if half == 0:
            send(cond & (row == 0), source, piece(head_ref, chunk), head_send.at[chunk],
                 head_sem.at[chunk], row + 1, col)
        mine = cond & (row == owner) & (part == half)
        send(mine & (row < row_count - 1), source, piece(column_ref, chunk), col_up.at[chunk],
             col_sem.at[chunk], row + 1, col)
        send(mine & (row > 0), source, piece(column_ref, chunk), col_down.at[chunk],
             col_sem.at[chunk], row - 1, col)

    always = row >= 0
    for half in range(halves):
        own = own_ref.at[half]
        go_side(half, col, own, always)
        go_up(half, col, own, always)
        go_down(half, col, own, always)
        pass_on(half, col, own, always)
    for half in range(halves):
        rows_ref[half, pl.ds(pl.multiple_of(col * width, 8), width), :] = own_ref[half]

    order = [(0, line, always)]
    for away in range(1, lines):
        order.append((away, jnp.maximum(line - away, 0), line >= away))
        order.append((-away, jnp.minimum(line + away, lines - 1), line + away < lines))

    def row_event(half, away, at, cond):
        chunk = at * 2 + side
        if away != 0:
            arrived(cond, slot(half, chunk), row_sem.at[half, chunk])
            (go_up if away > 0 else go_down)(half, chunk, slot(half, chunk), cond)
            go_side(half, chunk, slot(half, chunk), cond)
            pass_on(half, chunk, slot(half, chunk), cond)
        chunk = at * 2 + 1 - side
        arrived(cond, slot(half, chunk), row_sem.at[half, chunk])
        pass_on(half, chunk, slot(half, chunk), cond)

    def head_event(at, cond):
        for chunk in (at * 2 + side, at * 2 + 1 - side):
            taken = cond & (row > 0)
            arrived(taken, piece(head_ref, chunk), head_sem.at[chunk])
            send(taken & (row < row_count - 1), piece(head_ref, chunk), piece(head_ref, chunk),
                 head_send.at[chunk], head_sem.at[chunk], row + 1, col)

    def col_event(at, cond):
        for chunk in (at * 2 + side, at * 2 + 1 - side):
            arrived(cond & (row != owner), piece(column_ref, chunk), col_sem.at[chunk])
            send(cond & (row > owner) & (row < row_count - 1), piece(column_ref, chunk),
                 piece(column_ref, chunk), col_up.at[chunk], col_sem.at[chunk], row + 1, col)
            send(cond & (row < owner) & (row > 0), piece(column_ref, chunk),
                 piece(column_ref, chunk), col_down.at[chunk], col_sem.at[chunk], row - 1, col)

    for away, at, cond in order:
        row_event(0, away, at, cond)
    for away, at, cond in order:
        head_event(at, cond)

    @pl.when(row == 0)
    def _():
        head_ref[...] = rows_ref[0]

    events = [
        functools.partial(row_event, half, away, at, cond)
        for half in range(1, halves)
        for away, at, cond in order
    ] + [functools.partial(col_event, at, cond) for _, at, cond in order]
    turns = centers // LANES

    def beside(turn):
        for number in range(turns):

            @pl.when(turn == number)
            def _(number=number):
                for event in events[
                    len(events) * number // turns : len(events) * (number + 1) // turns
                ]:
                    event()

    step = 2 * LANES if head_ref.shape[0] % (2 * LANES) == 0 else LANES
    gauss_into(corner, head_ref, head_ref, 0, FINE, step)
    factor_into(corner, chol, inverse, work, block, done, beside)

    @pl.when(row == owner)
    def _():
        column_ref[...] = rows_ref[part]

    col_start = col * centers
    gauss_into(side_tile, column_ref, head_ref, col_start, PLAIN, step)
    far[...] = jnp.where(col == 0, 0.0, product(side_tile[...], inverse[...], 1, FINE))

    def finish(half, carry):
        first = (row * halves + half) * centers
        here = pl.ds(pl.multiple_of(half * centers, centers), centers)
        gauss_into(side_tile, rows_ref.at[half], head_ref, first, PLAIN, step)
        solved = product(side_tile[...], inverse[...], 1, FINE)
        top = first == 0
        panel_ref[here, :] = jnp.where(top, chol[...], solved)
        gauss_into(tile, rows_ref.at[half], column_ref, first - col_start, PLAIN, step)
        trail_ref[here, :] = tile[...] - product(
            jnp.where(top, 0.0, solved), far[...], 1, PLAIN
        )
        return carry

    lax.fori_loop(0, halves, finish, 0)

    def gone(cond, source, send_sem):
        pl.when(cond)(lambda: copy_of(source, source, send_sem, send_sem, row, col).wait_send())

    for away, at, cond in order:
        chunk = at * 2 + side
        for half in range(halves):
            gone(cond & (line < lines - 1) & (at <= line), slot(half, chunk), up_sem.at[half, chunk])
            gone(cond & (line > 0) & (at >= line), slot(half, chunk), down_sem.at[half, chunk])
            gone(cond, slot(half, chunk), side_sem.at[half, chunk])
        for chunk in (at * 2 + side, at * 2 + 1 - side):
            gone(cond & (row < row_count - 1), piece(head_ref, chunk), head_send.at[chunk])
            gone(cond & (row >= owner) & (row < row_count - 1), piece(column_ref, chunk), col_up.at[chunk])
            gone(cond & (row <= owner) & (row > 0), piece(column_ref, chunk), col_down.at[chunk])


def factor_panel(turned, row_count, col_count):
    halves, width, centers = turned.shape
    depth = width * col_count
    dma = pltpu.SemaphoreType.DMA
    square = pltpu.VMEM((centers, centers), jnp.float32)
    return pl.pallas_call(
        functools.partial(panel_kernel, row_count, col_count),
        out_shape=[jax.ShapeDtypeStruct((halves * centers, centers), jnp.float32)] * 2,
        in_specs=[pl.BlockSpec(memory_space=pltpu.VMEM)],
        out_specs=[pl.BlockSpec(memory_space=pltpu.VMEM)] * 2,
        scratch_shapes=[
            pltpu.VMEM((halves, depth, centers), jnp.float32),
            pltpu.VMEM((depth, centers), jnp.float32),
            pltpu.VMEM((depth, centers), jnp.float32),
            square,
            square,
            square,
            square,
            square,
            square,
            pltpu.VMEM((centers, 2 * centers), jnp.float32),
            pltpu.VMEM((LANES, 2 * LANES), jnp.float32),
            pltpu.VMEM((LANES, 2 * LANES), jnp.float32),
            dma((halves, col_count)),
            dma((col_count,)),
            dma((col_count,)),
            dma((halves, col_count)),
            dma((halves, col_count)),
            dma((halves, col_count)),
            dma((col_count,)),
            dma((col_count,)),
            dma((col_count,)),
        ],
        compiler_params=pltpu.CompilerParams(
            collective_id=0, has_side_effects=True, vmem_limit_bytes=56 * 1024 * 1024
        ),
        name="panel",
    )(turned)


def on_device(features):
    row_count = lax.axis_size("row")
    col_count = lax.axis_size("col")
    row_height, width = features.shape
    halves = col_count // row_count
    turned = features.reshape(halves, row_height // halves, width).transpose(0, 2, 1)
    return tuple(factor_panel(turned, row_count, col_count))


def solution(mesh):
    return jax.shard_map(
        on_device,
        mesh=mesh,
        in_specs=(P("row", "col"),),
        out_specs=(P("row", None), P("row", "col")),
        check_vma=False,
    )
```

```python
import functools

import jax
import jax.numpy as jnp
from jax import lax
from jax.experimental import pallas as pl
from jax.experimental.pallas import tpu as pltpu
from jax.sharding import PartitionSpec as P

D = 1536


gamma_scale = 0.6
ridge_value = 0.05

MESH = pl.DeviceIdType.MESH
LANES = 128
GROUP = 8


def split_three(value):
    high = value.astype(jnp.bfloat16).astype(jnp.float32)
    rest = value - high
    middle = rest.astype(jnp.bfloat16).astype(jnp.float32)
    return high, middle, rest - middle


def outer_update(rows_here):
    high, middle, low = split_three(rows_here)
    right = jnp.concatenate([high, middle, high, low, high, middle], axis=0).astype(jnp.bfloat16)
    left = jnp.concatenate(
        [part[:, :LANES] for part in (high, high, middle, high, low, middle)], axis=0
    ).astype(jnp.bfloat16)
    return lax.dot_general(
        left, right, (((0,), (0,)), ((), ())), preferred_element_type=jnp.float32
    )


def factor_group(block_ref, done_ref, first):
    left_rows = [block_ref[pl.ds(first + t, 1), pl.ds(0, LANES)] for t in range(GROUP)]
    right_rows = [block_ref[pl.ds(first + t, 1), pl.ds(LANES, LANES)] for t in range(GROUP)]
    entry = {}
    for i in range(GROUP):
        for t in range(i + 1):
            entry[i, t] = jnp.broadcast_to(
                left_rows[i][:, first + t : first + t + 1], (1, LANES)
            )
    for t in range(GROUP):
        scale = lax.rsqrt(entry[t, t])
        scale = scale * (1.5 - 0.5 * entry[t, t] * scale * scale)
        ratio = [None] * GROUP
        for i in range(t + 1, GROUP):
            ratio[i] = entry[i, t] * scale
        for i in range(t + 1, GROUP):
            for k in range(t + 1, i + 1):
                entry[i, k] = entry[i, k] - ratio[i] * ratio[k]
        left_rows[t] = left_rows[t] * scale
        right_rows[t] = right_rows[t] * scale
        for i in range(t + 1, GROUP):
            left_rows[i] = left_rows[i] - ratio[i] * left_rows[t]
            right_rows[i] = right_rows[i] - ratio[i] * right_rows[t]
    for t in range(GROUP):
        done_ref[pl.ds(first + t, 1), pl.ds(0, LANES)] = left_rows[t]
        done_ref[pl.ds(first + t, 1), pl.ds(LANES, LANES)] = right_rows[t]
    after = first + GROUP
    if after < LANES:
        change = outer_update(done_ref[pl.ds(first, GROUP), :])
        block_ref[pl.ds(after, LANES - after), :] -= change[after:, :]


def stacked(value, order, axis):
    parts = split_three(value)
    return jnp.concatenate([parts[at].astype(jnp.bfloat16) for at in order], axis=axis)


FINE = ((0, 0, 1, 0, 2, 1), (0, 1, 0, 2, 0, 1))
PLAIN = ((0, 0, 1), (0, 1, 0))


def product(left, right, axis, orders):
    return lax.dot_general(
        stacked(left, orders[0], axis),
        stacked(right, orders[1], axis),
        (((axis,), (axis,)), ((), ())),
        preferred_element_type=jnp.float32,
    )


def diagonal(rows, columns, offset):
    return (
        offset + lax.broadcasted_iota(jnp.int32, (rows, columns), 0)
        == lax.broadcasted_iota(jnp.int32, (rows, columns), 1)
    )


def gauss_into(out_ref, left, right, offset, orders, step, beside=None):
    depth, rows = left.shape
    columns = right.shape[1]
    out_ref[...] = jnp.zeros((rows, columns), jnp.float32)

    def add(at, squares):
        span = pl.ds(pl.multiple_of(at * step, step), step)
        one, two = left[span, :], right[span, :]
        out_ref[...] += product(one, two, 0, orders)
        if beside is not None:
            beside(at)
        return (
            squares[0] + jnp.sum(one * one, axis=0, keepdims=True),
            squares[1] + jnp.sum(two * two, axis=0, keepdims=True),
        )

    left_sq, right_sq = lax.fori_loop(
        0,
        depth // step,
        add,
        (jnp.zeros((1, rows), jnp.float32), jnp.zeros((1, columns), jnp.float32)),
    )
    left_sq = jnp.broadcast_to(left_sq, (LANES, rows)).T[:, :1]
    distance = left_sq + right_sq - 2.0 * out_ref[...]
    kernel_value = jnp.exp(-distance * (gamma_scale / D))
    out_ref[...] = kernel_value + jnp.where(
        diagonal(rows, columns, offset), ridge_value, 0.0
    )


def factor_into(corner_ref, chol_ref, inverse_ref, work, block, done, beside):
    size = corner_ref.shape[0]
    work[:, pl.ds(0, size)] = corner_ref[...]
    work[:, pl.ds(size, size)] = diagonal(size, size, 0).astype(jnp.float32)

    def step(at, carry):
        start = pl.multiple_of(at * LANES, LANES)
        rows = pl.ds(start, LANES)
        block[:, pl.ds(0, LANES)] = work[rows, rows]
        block[:, pl.ds(LANES, LANES)] = diagonal(LANES, LANES, 0).astype(jnp.float32)
        for first in range(0, LANES, GROUP):
            factor_group(block, done, first)
        solved = jnp.dot(
            done[:, pl.ds(LANES, LANES)],
            work[rows, :],
            precision=lax.Precision.HIGHEST,
            preferred_element_type=jnp.float32,
        )
        upper = solved[:, :size]
        keep = (
            start + lax.broadcasted_iota(jnp.int32, (LANES, size), 0)
            <= lax.broadcasted_iota(jnp.int32, (LANES, size), 1)
        )
        chol_ref[:, rows] = jnp.where(keep, upper, 0.0).T
        inverse_ref[rows, :] = solved[:, size:]
        for other in range(LANES, size, LANES):

            @pl.when(other > start)
            def _(other=other):
                across = chol_ref[pl.ds(other, LANES), rows]
                work[pl.ds(other, LANES), :] -= jnp.dot(
                    across,
                    solved,
                    precision=lax.Precision.HIGHEST,
                    preferred_element_type=jnp.float32,
                )

        beside(at)
        return carry

    lax.fori_loop(0, size // LANES, step, 0)


def panel_kernel(row_count, col_count, own_ref, panel_ref, trail_ref, rows_ref, head_ref, column_ref,
                 corner, chol, inverse, far, side_tiles, work, block, done, inverse_sem,
                 row_sem, head_sem, col_sem, up_sem, down_sem, side_sem, head_send, col_up, col_down):
    halves, width, centers = own_ref.shape
    row = lax.axis_index("row")
    col = lax.axis_index("col")
    lines = col_count // 2
    line, side = col // 2, col % 2
    owner = col // halves
    part = col % halves

    def copy_of(source, target, send_sem, recv_sem, to_row, to_col):
        return pltpu.make_async_remote_copy(
            src_ref=source,
            dst_ref=target,
            send_sem=send_sem,
            recv_sem=recv_sem,
            device_id=(to_row, to_col),
            device_id_type=MESH,
        )

    def arrived(cond, target, recv_sem):
        pl.when(cond)(lambda: copy_of(target, target, recv_sem, recv_sem, row, col).wait_recv())

    def send(cond, source, target, send_sem, recv_sem, to_row, to_col):
        pl.when(cond)(lambda: copy_of(source, target, send_sem, recv_sem, to_row, to_col).start())

    def slot(half, chunk):
        return rows_ref.at[half, pl.ds(pl.multiple_of(chunk * width, 8), width), :]

    def piece(ref, chunk):
        return ref.at[pl.ds(pl.multiple_of(chunk * width, 8), width), :]

    neighbours = (
        (line < lines - 1, row, col + 2),
        (line > 0, row, col - 2),
        (row >= 0, row, line * 2 + 1 - side),
        (row < row_count - 1, row + 1, col),
        (row > 0, row - 1, col),
    )
    barrier = pltpu.get_barrier_semaphore()
    for cond, to_row, to_col in neighbours:
        pl.when(cond)(
            lambda to_row=to_row, to_col=to_col: pl.semaphore_signal(
                barrier, inc=1, device_id=(to_row, to_col), device_id_type=MESH
            )
        )
    pl.semaphore_wait(barrier, sum(cond.astype(jnp.int32) for cond, _, _ in neighbours))

    def go_up(half, chunk, source, cond):
        send(cond & (line < lines - 1), source, slot(half, chunk), up_sem.at[half, chunk],
             row_sem.at[half, chunk], row, col + 2)

    def go_down(half, chunk, source, cond):
        send(cond & (line > 0), source, slot(half, chunk), down_sem.at[half, chunk],
             row_sem.at[half, chunk], row, col - 2)

    def go_side(half, chunk, source, cond):
        send(cond, source, slot(half, chunk), side_sem.at[half, chunk],
             row_sem.at[half, chunk], row, line * 2 + 1 - side)

    def pass_on(half, chunk, source, cond):
        if half == 0:
            send(cond & (row == 0), source, piece(head_ref, chunk), head_send.at[chunk],
                 head_sem.at[chunk], row + 1, col)
        mine = cond & (row == owner) & (part == half)
        send(mine & (row < row_count - 1), source, piece(column_ref, chunk), col_up.at[chunk],
             col_sem.at[chunk], row + 1, col)
        send(mine & (row > 0), source, piece(column_ref, chunk), col_down.at[chunk],
             col_sem.at[chunk], row - 1, col)

    always = row >= 0
    for half in range(halves):
        own = own_ref.at[half]
        go_side(half, col, own, always)
        go_up(half, col, own, always)
        go_down(half, col, own, always)
        pass_on(half, col, own, always)
    for half in range(halves):
        rows_ref[half, pl.ds(pl.multiple_of(col * width, 8), width), :] = own_ref[half]

    order = [(0, line, always)]
    for away in range(1, lines):
        order.append((away, jnp.maximum(line - away, 0), line >= away))
        order.append((-away, jnp.minimum(line + away, lines - 1), line + away < lines))

    def row_event(half, away, at, cond):
        chunk = at * 2 + side
        if away != 0:
            arrived(cond, slot(half, chunk), row_sem.at[half, chunk])
            (go_up if away > 0 else go_down)(half, chunk, slot(half, chunk), cond)
            go_side(half, chunk, slot(half, chunk), cond)
            pass_on(half, chunk, slot(half, chunk), cond)
        chunk = at * 2 + 1 - side
        arrived(cond, slot(half, chunk), row_sem.at[half, chunk])
        pass_on(half, chunk, slot(half, chunk), cond)

    def head_event(at, cond):
        for chunk in (at * 2 + side, at * 2 + 1 - side):
            taken = cond & (row > 0)
            arrived(taken, piece(head_ref, chunk), head_sem.at[chunk])
            send(taken & (row < row_count - 1), piece(head_ref, chunk), piece(head_ref, chunk),
                 head_send.at[chunk], head_sem.at[chunk], row + 1, col)

    def col_event(at, cond):
        for chunk in (at * 2 + side, at * 2 + 1 - side):
            arrived(cond & (row != owner), piece(column_ref, chunk), col_sem.at[chunk])
            send(cond & (row > owner) & (row < row_count - 1), piece(column_ref, chunk),
                 piece(column_ref, chunk), col_up.at[chunk], col_sem.at[chunk], row + 1, col)
            send(cond & (row < owner) & (row > 0), piece(column_ref, chunk),
                 piece(column_ref, chunk), col_down.at[chunk], col_sem.at[chunk], row - 1, col)

    for away, at, cond in order:
        row_event(0, away, at, cond)
    rest = [
        functools.partial(row_event, half, away, at, cond)
        for half in range(1, halves)
        for away, at, cond in order
    ]
    heads = [functools.partial(head_event, at, cond) for _, at, cond in order]
    columns = [functools.partial(col_event, at, cond) for _, at, cond in order]

    def among(events, turns):
        def beside(turn):
            for number in range(turns):

                @pl.when(turn == number)
                def _(number=number):
                    for event in events[
                        len(events) * number // turns : len(events) * (number + 1) // turns
                    ]:
                        event()

        return beside

    depth = head_ref.shape[0]
    step = 2 * LANES if depth % (2 * LANES) == 0 else LANES
    col_start = col * centers
    first_row = row * halves * centers

    def send_inverse(cond):
        send(cond & (row < row_count - 1), inverse, inverse, inverse_sem.at[0], inverse_sem.at[1],
             row + 1, col)

    @pl.when(row == 0)
    def _():
        head_ref[...] = rows_ref[0]
        gauss_into(corner, head_ref, head_ref, 0, FINE, step)
        factor_into(corner, chol, inverse, work, block, done, among(rest + columns, centers // LANES))
        send_inverse(always)

    @pl.when(row > 0)
    def _():
        for number, event in enumerate(rest):
            event()
            if number < len(heads):
                heads[number]()
        for event in heads[len(rest):]:
            event()
        gauss_into(side_tiles.at[0], rows_ref.at[0], head_ref, first_row, PLAIN, step,
                   among(columns, depth // step))

    @pl.when(row == owner)
    def _():
        column_ref[...] = rows_ref[part]

    def side_of(half, carry):
        gauss_into(side_tiles.at[half], rows_ref.at[half], head_ref, first_row + half * centers, PLAIN, step)
        return carry

    def tile_of(half, carry):
        here = pl.ds(pl.multiple_of(half * centers, centers), centers)
        gauss_into(trail_ref.at[here, :], rows_ref.at[half], column_ref,
                   first_row + half * centers - col_start, PLAIN, step)
        return carry

    lax.fori_loop(1, halves, side_of, 0)
    lax.fori_loop(0, halves, tile_of, 0)
    gauss_into(far, column_ref, head_ref, col_start, PLAIN, step)

    arrived(row > 0, inverse, inverse_sem.at[1])
    send_inverse(row > 0)
    far[...] = jnp.where(col == 0, 0.0, product(far[...], inverse[...], 1, FINE))

    def finish(half, carry):
        here = pl.ds(pl.multiple_of(half * centers, centers), centers)
        solved = product(side_tiles[half], inverse[...], 1, FINE)
        panel_ref[here, :] = solved
        trail_ref[here, :] -= product(solved, far[...], 1, PLAIN)
        return carry

    lax.fori_loop(jnp.where(row == 0, 1, 0), halves, finish, 0)

    @pl.when(row == 0)
    def _():
        panel_ref[pl.ds(0, centers), :] = chol[...]

    def gone(cond, source, send_sem):
        pl.when(cond)(lambda: copy_of(source, source, send_sem, send_sem, row, col).wait_send())

    gone(row < row_count - 1, inverse, inverse_sem.at[0])
    for away, at, cond in order:
        chunk = at * 2 + side
        for half in range(halves):
            gone(cond & (line < lines - 1) & (at <= line), slot(half, chunk), up_sem.at[half, chunk])
            gone(cond & (line > 0) & (at >= line), slot(half, chunk), down_sem.at[half, chunk])
            gone(cond, slot(half, chunk), side_sem.at[half, chunk])
        for chunk in (at * 2 + side, at * 2 + 1 - side):
            gone(cond & (row < row_count - 1), piece(head_ref, chunk), head_send.at[chunk])
            gone(cond & (row >= owner) & (row < row_count - 1), piece(column_ref, chunk), col_up.at[chunk])
            gone(cond & (row <= owner) & (row > 0), piece(column_ref, chunk), col_down.at[chunk])


def factor_panel(turned, row_count, col_count):
    halves, width, centers = turned.shape
    depth = width * col_count
    dma = pltpu.SemaphoreType.DMA
    square = pltpu.VMEM((centers, centers), jnp.float32)
    return pl.pallas_call(
        functools.partial(panel_kernel, row_count, col_count),
        out_shape=[jax.ShapeDtypeStruct((halves * centers, centers), jnp.float32)] * 2,
        in_specs=[pl.BlockSpec(memory_space=pltpu.VMEM)],
        out_specs=[pl.BlockSpec(memory_space=pltpu.VMEM)] * 2,
        scratch_shapes=[
            pltpu.VMEM((halves, depth, centers), jnp.float32),
            pltpu.VMEM((depth, centers), jnp.float32),
            pltpu.VMEM((depth, centers), jnp.float32),
            square,
            square,
            square,
            square,
            pltpu.VMEM((halves, centers, centers), jnp.float32),
            pltpu.VMEM((centers, 2 * centers), jnp.float32),
            pltpu.VMEM((LANES, 2 * LANES), jnp.float32),
            pltpu.VMEM((LANES, 2 * LANES), jnp.float32),
            dma((2,)),
            dma((halves, col_count)),
            dma((col_count,)),
            dma((col_count,)),
            dma((halves, col_count)),
            dma((halves, col_count)),
            dma((halves, col_count)),
            dma((col_count,)),
            dma((col_count,)),
            dma((col_count,)),
        ],
        compiler_params=pltpu.CompilerParams(
            collective_id=0, has_side_effects=True, vmem_limit_bytes=56 * 1024 * 1024
        ),
        name="panel",
    )(turned)


def on_device(features):
    row_count = lax.axis_size("row")
    col_count = lax.axis_size("col")
    row_height, width = features.shape
    halves = col_count // row_count
    turned = features.reshape(halves, row_height // halves, width).transpose(0, 2, 1)
    return tuple(factor_panel(turned, row_count, col_count))


def solution(mesh):
    return jax.shard_map(
        on_device,
        mesh=mesh,
        in_specs=(P("row", "col"),),
        out_specs=(P("row", None), P("row", "col")),
        check_vma=False,
    )
```

```python
import functools

import jax
import jax.numpy as jnp
from jax import lax
from jax.experimental import pallas as pl
from jax.experimental.pallas import tpu as pltpu
from jax.sharding import PartitionSpec as P

D = 1536


gamma_scale = 0.6
ridge_value = 0.05

MESH = pl.DeviceIdType.MESH
LANES = 128
GROUP = 8


def split_three(value):
    high = value.astype(jnp.bfloat16).astype(jnp.float32)
    rest = value - high
    middle = rest.astype(jnp.bfloat16).astype(jnp.float32)
    return high, middle, rest - middle


def outer_update(rows_here):
    high, middle, low = split_three(rows_here)
    right = jnp.concatenate([high, middle, high, low, high, middle], axis=0).astype(jnp.bfloat16)
    left = jnp.concatenate(
        [part[:, :LANES] for part in (high, high, middle, high, low, middle)], axis=0
    ).astype(jnp.bfloat16)
    return lax.dot_general(
        left, right, (((0,), (0,)), ((), ())), preferred_element_type=jnp.float32
    )


def factor_group(block_ref, done_ref, first):
    left_rows = [block_ref[pl.ds(first + t, 1), pl.ds(0, LANES)] for t in range(GROUP)]
    right_rows = [block_ref[pl.ds(first + t, 1), pl.ds(LANES, LANES)] for t in range(GROUP)]
    entry = {}
    for i in range(GROUP):
        for t in range(i + 1):
            entry[i, t] = jnp.broadcast_to(
                left_rows[i][:, first + t : first + t + 1], (1, LANES)
            )
    for t in range(GROUP):
        scale = lax.rsqrt(entry[t, t])
        scale = scale * (1.5 - 0.5 * entry[t, t] * scale * scale)
        ratio = [None] * GROUP
        for i in range(t + 1, GROUP):
            ratio[i] = entry[i, t] * scale
        for i in range(t + 1, GROUP):
            for k in range(t + 1, i + 1):
                entry[i, k] = entry[i, k] - ratio[i] * ratio[k]
        left_rows[t] = left_rows[t] * scale
        right_rows[t] = right_rows[t] * scale
        for i in range(t + 1, GROUP):
            left_rows[i] = left_rows[i] - ratio[i] * left_rows[t]
            right_rows[i] = right_rows[i] - ratio[i] * right_rows[t]
    for t in range(GROUP):
        done_ref[pl.ds(first + t, 1), pl.ds(0, LANES)] = left_rows[t]
        done_ref[pl.ds(first + t, 1), pl.ds(LANES, LANES)] = right_rows[t]
    after = first + GROUP
    if after < LANES:
        change = outer_update(done_ref[pl.ds(first, GROUP), :])
        block_ref[pl.ds(after, LANES - after), :] -= change[after:, :]


def stacked(value, order, axis):
    parts = split_three(value)
    return jnp.concatenate([parts[at].astype(jnp.bfloat16) for at in order], axis=axis)


FINE = ((0, 0, 1, 0, 2, 1), (0, 1, 0, 2, 0, 1))
PLAIN = ((0, 0, 1), (0, 1, 0))


def product(left, right, axis, orders):
    return lax.dot_general(
        stacked(left, orders[0], axis),
        stacked(right, orders[1], axis),
        (((axis,), (axis,)), ((), ())),
        preferred_element_type=jnp.float32,
    )


def diagonal(rows, columns, offset):
    return (
        offset + lax.broadcasted_iota(jnp.int32, (rows, columns), 0)
        == lax.broadcasted_iota(jnp.int32, (rows, columns), 1)
    )


def gauss_into(out_ref, left, right, offset, orders, step, beside=None):
    depth, rows = left.shape
    columns = right.shape[1]
    out_ref[...] = jnp.zeros((rows, columns), jnp.float32)

    def add(at, squares):
        span = pl.ds(pl.multiple_of(at * step, step), step)
        one, two = left[span, :], right[span, :]
        out_ref[...] += product(one, two, 0, orders)
        if beside is not None:
            beside(at)
        return (
            squares[0] + jnp.sum(one * one, axis=0, keepdims=True),
            squares[1] + jnp.sum(two * two, axis=0, keepdims=True),
        )

    left_sq, right_sq = lax.fori_loop(
        0,
        depth // step,
        add,
        (jnp.zeros((1, rows), jnp.float32), jnp.zeros((1, columns), jnp.float32)),
    )
    left_sq = jnp.broadcast_to(left_sq, (LANES, rows)).T[:, :1]
    distance = left_sq + right_sq - 2.0 * out_ref[...]
    kernel_value = jnp.exp(-distance * (gamma_scale / D))
    out_ref[...] = kernel_value + jnp.where(
        diagonal(rows, columns, offset), ridge_value, 0.0
    )


def factor_into(corner_ref, chol_ref, inverse_ref, work, block, done, beside):
    size = corner_ref.shape[0]
    work[:, pl.ds(0, size)] = corner_ref[...]
    work[:, pl.ds(size, size)] = diagonal(size, size, 0).astype(jnp.float32)

    def step(at, carry):
        start = pl.multiple_of(at * LANES, LANES)
        rows = pl.ds(start, LANES)
        block[:, pl.ds(0, LANES)] = work[rows, rows]
        block[:, pl.ds(LANES, LANES)] = diagonal(LANES, LANES, 0).astype(jnp.float32)
        for first in range(0, LANES, GROUP):
            factor_group(block, done, first)
        solved = jnp.dot(
            done[:, pl.ds(LANES, LANES)],
            work[rows, :],
            precision=lax.Precision.HIGHEST,
            preferred_element_type=jnp.float32,
        )
        upper = solved[:, :size]
        keep = (
            start + lax.broadcasted_iota(jnp.int32, (LANES, size), 0)
            <= lax.broadcasted_iota(jnp.int32, (LANES, size), 1)
        )
        chol_ref[:, rows] = jnp.where(keep, upper, 0.0).T
        inverse_ref[rows, :] = solved[:, size:]
        for other in range(LANES, size, LANES):

            @pl.when(other > start)
            def _(other=other):
                across = chol_ref[pl.ds(other, LANES), rows]
                work[pl.ds(other, LANES), :] -= jnp.dot(
                    across,
                    solved,
                    precision=lax.Precision.HIGHEST,
                    preferred_element_type=jnp.float32,
                )

        beside(at)
        return carry

    lax.fori_loop(0, size // LANES, step, 0)


def panel_kernel(row_count, col_count, own_ref, panel_ref, trail_ref, rows_ref, head_ref, column_ref,
                 corner, chol, inverse, far, side_tiles, work, block, done, inverse_sem,
                 row_sem, head_sem, col_sem, up_sem, down_sem, side_sem, head_send, col_up, col_down):
    halves, width, centers = own_ref.shape
    row = lax.axis_index("row")
    col = lax.axis_index("col")
    lines = col_count // 2
    line, side = col // 2, col % 2
    owner = col // halves
    part = col % halves

    def copy_of(source, target, send_sem, recv_sem, to_row, to_col):
        return pltpu.make_async_remote_copy(
            src_ref=source,
            dst_ref=target,
            send_sem=send_sem,
            recv_sem=recv_sem,
            device_id=(to_row, to_col),
            device_id_type=MESH,
        )

    def arrived(cond, target, recv_sem):
        pl.when(cond)(lambda: copy_of(target, target, recv_sem, recv_sem, row, col).wait_recv())

    def send(cond, source, target, send_sem, recv_sem, to_row, to_col):
        pl.when(cond)(lambda: copy_of(source, target, send_sem, recv_sem, to_row, to_col).start())

    def slot(half, chunk):
        return rows_ref.at[half, pl.ds(pl.multiple_of(chunk * width, 8), width), :]

    def piece(ref, chunk):
        return ref.at[pl.ds(pl.multiple_of(chunk * width, 8), width), :]

    neighbours = (
        (line < lines - 1, row, col + 2),
        (line > 0, row, col - 2),
        (row >= 0, row, line * 2 + 1 - side),
        (row < row_count - 1, row + 1, col),
        (row > 0, row - 1, col),
    )
    barrier = pltpu.get_barrier_semaphore()
    for cond, to_row, to_col in neighbours:
        pl.when(cond)(
            lambda to_row=to_row, to_col=to_col: pl.semaphore_signal(
                barrier, inc=1, device_id=(to_row, to_col), device_id_type=MESH
            )
        )
    pl.semaphore_wait(barrier, sum(cond.astype(jnp.int32) for cond, _, _ in neighbours))

    def go_up(half, chunk, source, cond):
        send(cond & (line < lines - 1), source, slot(half, chunk), up_sem.at[half, chunk],
             row_sem.at[half, chunk], row, col + 2)

    def go_down(half, chunk, source, cond):
        send(cond & (line > 0), source, slot(half, chunk), down_sem.at[half, chunk],
             row_sem.at[half, chunk], row, col - 2)

    def go_side(half, chunk, source, cond):
        send(cond, source, slot(half, chunk), side_sem.at[half, chunk],
             row_sem.at[half, chunk], row, line * 2 + 1 - side)

    def pass_on(half, chunk, source, cond):
        if half == 0:
            send(cond & (row == 0), source, piece(head_ref, chunk), head_send.at[chunk],
                 head_sem.at[chunk], row + 1, col)
        mine = cond & (row == owner) & (part == half)
        send(mine & (row < row_count - 1), source, piece(column_ref, chunk), col_up.at[chunk],
             col_sem.at[chunk], row + 1, col)
        send(mine & (row > 0), source, piece(column_ref, chunk), col_down.at[chunk],
             col_sem.at[chunk], row - 1, col)

    always = row >= 0

    def own_sends(half):
        own = own_ref.at[half]
        go_side(half, col, own, always)
        go_up(half, col, own, always)
        go_down(half, col, own, always)
        pass_on(half, col, own, always)

    own_sends(0)
    for half in range(halves):
        rows_ref[half, pl.ds(pl.multiple_of(col * width, 8), width), :] = own_ref[half]

    order = [(0, line, always)]
    for away in range(1, lines):
        order.append((away, jnp.maximum(line - away, 0), line >= away))
        order.append((-away, jnp.minimum(line + away, lines - 1), line + away < lines))

    def row_event(half, away, at, cond):
        chunk = at * 2 + side
        if away != 0:
            arrived(cond, slot(half, chunk), row_sem.at[half, chunk])
            (go_up if away > 0 else go_down)(half, chunk, slot(half, chunk), cond)
            go_side(half, chunk, slot(half, chunk), cond)
            pass_on(half, chunk, slot(half, chunk), cond)
        chunk = at * 2 + 1 - side
        arrived(cond, slot(half, chunk), row_sem.at[half, chunk])
        pass_on(half, chunk, slot(half, chunk), cond)

    def head_event(at, cond):
        for chunk in (at * 2 + side, at * 2 + 1 - side):
            taken = cond & (row > 0)
            arrived(taken, piece(head_ref, chunk), head_sem.at[chunk])
            send(taken & (row < row_count - 1), piece(head_ref, chunk), piece(head_ref, chunk),
                 head_send.at[chunk], head_sem.at[chunk], row + 1, col)

    def col_event(at, cond):
        for chunk in (at * 2 + side, at * 2 + 1 - side):
            arrived(cond & (row != owner), piece(column_ref, chunk), col_sem.at[chunk])
            send(cond & (row > owner) & (row < row_count - 1), piece(column_ref, chunk),
                 piece(column_ref, chunk), col_up.at[chunk], col_sem.at[chunk], row + 1, col)
            send(cond & (row < owner) & (row > 0), piece(column_ref, chunk),
                 piece(column_ref, chunk), col_down.at[chunk], col_sem.at[chunk], row - 1, col)

    for number, (away, at, cond) in enumerate(order):
        row_event(0, away, at, cond)
        if number == min(2, len(order) - 1):
            for half in range(1, halves):
                own_sends(half)
    rest = [
        functools.partial(row_event, half, away, at, cond)
        for half in range(1, halves)
        for away, at, cond in order
    ]
    heads = [functools.partial(head_event, at, cond) for _, at, cond in order]
    columns = [functools.partial(col_event, at, cond) for _, at, cond in order]

    def among(events, turns):
        def beside(turn):
            for number in range(turns):

                @pl.when(turn == number)
                def _(number=number):
                    for event in events[
                        len(events) * number // turns : len(events) * (number + 1) // turns
                    ]:
                        event()

        return beside

    depth = head_ref.shape[0]
    step = 2 * LANES if depth % (2 * LANES) == 0 else LANES
    col_start = col * centers
    first_row = row * halves * centers

    def send_inverse(cond):
        send(cond & (row < row_count - 1), inverse, inverse, inverse_sem.at[0], inverse_sem.at[1],
             row + 1, col)

    @pl.when(row == 0)
    def _():
        head_ref[...] = rows_ref[0]
        gauss_into(corner, head_ref, head_ref, 0, FINE, step)
        slots = centers // LANES
        late = [lambda: None] * (len(rest) // (slots - 1))
        factor_into(corner, chol, inverse, work, block, done, among(late + rest, slots))
        send_inverse(always)

    @pl.when(row > 0)
    def _():
        for event in heads:
            event()
        gauss_into(side_tiles.at[0], rows_ref.at[0], head_ref, first_row, PLAIN, step,
                   among(rest, depth // step))

    if halves == 1:
        for event in columns:
            event()
    else:
        gauss_into(side_tiles.at[1], rows_ref.at[1], head_ref, first_row + centers, PLAIN, step,
                   among(columns, depth // step))

    @pl.when(row == owner)
    def _():
        column_ref[...] = rows_ref[part]

    def side_of(half, carry):
        gauss_into(side_tiles.at[half], rows_ref.at[half], head_ref, first_row + half * centers, PLAIN, step)
        return carry

    def tile_of(half, carry):
        here = pl.ds(pl.multiple_of(half * centers, centers), centers)
        gauss_into(trail_ref.at[here, :], rows_ref.at[half], column_ref,
                   first_row + half * centers - col_start, PLAIN, step)
        return carry

    lax.fori_loop(2, halves, side_of, 0)
    lax.fori_loop(0, halves, tile_of, 0)
    gauss_into(far, column_ref, head_ref, col_start, PLAIN, step)

    arrived(row > 0, inverse, inverse_sem.at[1])
    send_inverse(row > 0)
    far[...] = jnp.where(col == 0, 0.0, product(far[...], inverse[...], 1, FINE))

    def finish(half, carry):
        here = pl.ds(pl.multiple_of(half * centers, centers), centers)
        solved = product(side_tiles[half], inverse[...], 1, FINE)
        panel_ref[here, :] = solved
        trail_ref[here, :] -= product(solved, far[...], 1, PLAIN)
        return carry

    lax.fori_loop(jnp.where(row == 0, 1, 0), halves, finish, 0)

    @pl.when(row == 0)
    def _():
        panel_ref[pl.ds(0, centers), :] = chol[...]

    def gone(cond, source, send_sem):
        pl.when(cond)(lambda: copy_of(source, source, send_sem, send_sem, row, col).wait_send())

    gone(row < row_count - 1, inverse, inverse_sem.at[0])
    for away, at, cond in order:
        chunk = at * 2 + side
        for half in range(halves):
            gone(cond & (line < lines - 1) & (at <= line), slot(half, chunk), up_sem.at[half, chunk])
            gone(cond & (line > 0) & (at >= line), slot(half, chunk), down_sem.at[half, chunk])
            gone(cond, slot(half, chunk), side_sem.at[half, chunk])
        for chunk in (at * 2 + side, at * 2 + 1 - side):
            gone(cond & (row < row_count - 1), piece(head_ref, chunk), head_send.at[chunk])
            gone(cond & (row >= owner) & (row < row_count - 1), piece(column_ref, chunk), col_up.at[chunk])
            gone(cond & (row <= owner) & (row > 0), piece(column_ref, chunk), col_down.at[chunk])


def factor_panel(turned, row_count, col_count):
    halves, width, centers = turned.shape
    depth = width * col_count
    dma = pltpu.SemaphoreType.DMA
    square = pltpu.VMEM((centers, centers), jnp.float32)
    return pl.pallas_call(
        functools.partial(panel_kernel, row_count, col_count),
        out_shape=[jax.ShapeDtypeStruct((halves * centers, centers), jnp.float32)] * 2,
        in_specs=[pl.BlockSpec(memory_space=pltpu.VMEM)],
        out_specs=[pl.BlockSpec(memory_space=pltpu.VMEM)] * 2,
        scratch_shapes=[
            pltpu.VMEM((halves, depth, centers), jnp.float32),
            pltpu.VMEM((depth, centers), jnp.float32),
            pltpu.VMEM((depth, centers), jnp.float32),
            square,
            square,
            square,
            square,
            pltpu.VMEM((halves, centers, centers), jnp.float32),
            pltpu.VMEM((centers, 2 * centers), jnp.float32),
            pltpu.VMEM((LANES, 2 * LANES), jnp.float32),
            pltpu.VMEM((LANES, 2 * LANES), jnp.float32),
            dma((2,)),
            dma((halves, col_count)),
            dma((col_count,)),
            dma((col_count,)),
            dma((halves, col_count)),
            dma((halves, col_count)),
            dma((halves, col_count)),
            dma((col_count,)),
            dma((col_count,)),
            dma((col_count,)),
        ],
        compiler_params=pltpu.CompilerParams(
            collective_id=0, has_side_effects=True, vmem_limit_bytes=56 * 1024 * 1024
        ),
        name="panel",
    )(turned)


def on_device(features):
    row_count = lax.axis_size("row")
    col_count = lax.axis_size("col")
    row_height, width = features.shape
    halves = col_count // row_count
    turned = features.reshape(halves, row_height // halves, width).transpose(0, 2, 1)
    return tuple(factor_panel(turned, row_count, col_count))


def solution(mesh):
    return jax.shard_map(
        on_device,
        mesh=mesh,
        in_specs=(P("row", "col"),),
        out_specs=(P("row", None), P("row", "col")),
        check_vma=False,
    )
```

```python
import functools

import jax
import jax.numpy as jnp
from jax import lax
from jax.experimental import pallas as pl
from jax.experimental.pallas import tpu as pltpu
from jax.sharding import PartitionSpec as P

D = 1536


gamma_scale = 0.6
ridge_value = 0.05

MESH = pl.DeviceIdType.MESH
LANES = 128
GROUP = 8


def split_three(value):
    high = value.astype(jnp.bfloat16).astype(jnp.float32)
    rest = value - high
    middle = rest.astype(jnp.bfloat16).astype(jnp.float32)
    return high, middle, rest - middle


def outer_update(rows_here):
    high, middle, low = split_three(rows_here)
    right = jnp.concatenate([high, middle, high, low, high, middle], axis=0).astype(jnp.bfloat16)
    left = jnp.concatenate(
        [part[:, :LANES] for part in (high, high, middle, high, low, middle)], axis=0
    ).astype(jnp.bfloat16)
    return lax.dot_general(
        left, right, (((0,), (0,)), ((), ())), preferred_element_type=jnp.float32
    )


def factor_group(block_ref, done_ref, first):
    left_rows = [block_ref[pl.ds(first + t, 1), pl.ds(0, LANES)] for t in range(GROUP)]
    right_rows = [block_ref[pl.ds(first + t, 1), pl.ds(LANES, LANES)] for t in range(GROUP)]
    entry = {}
    for i in range(GROUP):
        for t in range(i + 1):
            entry[i, t] = jnp.broadcast_to(
                left_rows[i][:, first + t : first + t + 1], (1, LANES)
            )
    for t in range(GROUP):
        scale = lax.rsqrt(entry[t, t])
        scale = scale * (1.5 - 0.5 * entry[t, t] * scale * scale)
        ratio = [None] * GROUP
        for i in range(t + 1, GROUP):
            ratio[i] = entry[i, t] * scale
        for i in range(t + 1, GROUP):
            for k in range(t + 1, i + 1):
                entry[i, k] = entry[i, k] - ratio[i] * ratio[k]
        left_rows[t] = left_rows[t] * scale
        right_rows[t] = right_rows[t] * scale
        for i in range(t + 1, GROUP):
            left_rows[i] = left_rows[i] - ratio[i] * left_rows[t]
            right_rows[i] = right_rows[i] - ratio[i] * right_rows[t]
    for t in range(GROUP):
        done_ref[pl.ds(first + t, 1), pl.ds(0, LANES)] = left_rows[t]
        done_ref[pl.ds(first + t, 1), pl.ds(LANES, LANES)] = right_rows[t]
    after = first + GROUP
    if after < LANES:
        change = outer_update(done_ref[pl.ds(first, GROUP), :])
        block_ref[pl.ds(after, LANES - after), :] -= change[after:, :]


def stacked(value, order, axis):
    parts = split_three(value)
    return jnp.concatenate([parts[at].astype(jnp.bfloat16) for at in order], axis=axis)


FINE = ((0, 0, 1, 0, 2, 1), (0, 1, 0, 2, 0, 1))
PLAIN = ((0, 0, 1), (0, 1, 0))


def product(left, right, axis, orders):
    return lax.dot_general(
        stacked(left, orders[0], axis),
        stacked(right, orders[1], axis),
        (((axis,), (axis,)), ((), ())),
        preferred_element_type=jnp.float32,
    )


def diagonal(rows, columns, offset):
    return (
        offset + lax.broadcasted_iota(jnp.int32, (rows, columns), 0)
        == lax.broadcasted_iota(jnp.int32, (rows, columns), 1)
    )


def gauss_into(out_ref, left, right, offset, orders, step, beside=None):
    depth, rows = left.shape
    columns = right.shape[1]
    out_ref[...] = jnp.zeros((rows, columns), jnp.float32)

    def add(at, squares):
        span = pl.ds(pl.multiple_of(at * step, step), step)
        one, two = left[span, :], right[span, :]
        out_ref[...] += product(one, two, 0, orders)
        if beside is not None:
            beside(at)
        return (
            squares[0] + jnp.sum(one * one, axis=0, keepdims=True),
            squares[1] + jnp.sum(two * two, axis=0, keepdims=True),
        )

    left_sq, right_sq = lax.fori_loop(
        0,
        depth // step,
        add,
        (jnp.zeros((1, rows), jnp.float32), jnp.zeros((1, columns), jnp.float32)),
    )
    left_sq = jnp.broadcast_to(left_sq, (LANES, rows)).T[:, :1]
    distance = left_sq + right_sq - 2.0 * out_ref[...]
    kernel_value = jnp.exp(-distance * (gamma_scale / D))
    out_ref[...] = kernel_value + jnp.where(
        diagonal(rows, columns, offset), ridge_value, 0.0
    )


def factor_into(corner_ref, chol_ref, inverse_ref, work, block, done, beside):
    size = corner_ref.shape[0]
    work[:, pl.ds(0, size)] = corner_ref[...]
    work[:, pl.ds(size, size)] = diagonal(size, size, 0).astype(jnp.float32)

    def step(at, carry):
        start = pl.multiple_of(at * LANES, LANES)
        rows = pl.ds(start, LANES)
        block[:, pl.ds(0, LANES)] = work[rows, rows]
        block[:, pl.ds(LANES, LANES)] = diagonal(LANES, LANES, 0).astype(jnp.float32)
        for first in range(0, LANES, GROUP):
            factor_group(block, done, first)
        solved = jnp.dot(
            done[:, pl.ds(LANES, LANES)],
            work[rows, :],
            precision=lax.Precision.HIGHEST,
            preferred_element_type=jnp.float32,
        )
        upper = solved[:, :size]
        keep = (
            start + lax.broadcasted_iota(jnp.int32, (LANES, size), 0)
            <= lax.broadcasted_iota(jnp.int32, (LANES, size), 1)
        )
        chol_ref[:, rows] = jnp.where(keep, upper, 0.0).T
        inverse_ref[rows, :] = solved[:, size:]
        for other in range(LANES, size, LANES):

            @pl.when(other > start)
            def _(other=other):
                across = chol_ref[pl.ds(other, LANES), rows]
                work[pl.ds(other, LANES), :] -= jnp.dot(
                    across,
                    solved,
                    precision=lax.Precision.HIGHEST,
                    preferred_element_type=jnp.float32,
                )

        beside(at)
        return carry

    lax.fori_loop(0, size // LANES, step, 0)


def panel_kernel(row_count, col_count, own_ref, panel_ref, trail_ref, rows_ref, head_ref, column_ref,
                 corner, chol, inverse, far, side_tiles, work, block, done, inverse_sem,
                 row_sem, head_sem, col_sem, up_sem, down_sem, side_sem, head_up, head_mate,
                 col_up, col_down, col_mate):
    halves, width, centers = own_ref.shape
    row = lax.axis_index("row")
    col = lax.axis_index("col")
    lines = col_count // 2
    line, side = col // 2, col % 2
    owner = col // halves
    part = col % halves
    mate = row + 1 - row % 2 * 2

    def copy_of(source, target, send_sem, recv_sem, to_row, to_col):
        return pltpu.make_async_remote_copy(
            src_ref=source,
            dst_ref=target,
            send_sem=send_sem,
            recv_sem=recv_sem,
            device_id=(to_row, to_col),
            device_id_type=MESH,
        )

    def arrived(cond, target, recv_sem):
        pl.when(cond)(lambda: copy_of(target, target, recv_sem, recv_sem, row, col).wait_recv())

    def send(cond, source, target, send_sem, recv_sem, to_row, to_col):
        pl.when(cond)(lambda: copy_of(source, target, send_sem, recv_sem, to_row, to_col).start())

    def slot(half, chunk):
        return rows_ref.at[half, pl.ds(pl.multiple_of(chunk * width, 8), width), :]

    def piece(ref, chunk):
        return ref.at[pl.ds(pl.multiple_of(chunk * width, 8), width), :]

    neighbours = (
        (line < lines - 1, row, col + 2),
        (line > 0, row, col - 2),
        (row >= 0, row, line * 2 + 1 - side),
        (row >= 0, mate, col),
        (row < row_count - 2, row + 2, col),
        (row > 1, row - 2, col),
    )
    barrier = pltpu.get_barrier_semaphore()
    for cond, to_row, to_col in neighbours:
        pl.when(cond)(
            lambda to_row=to_row, to_col=to_col: pl.semaphore_signal(
                barrier, inc=1, device_id=(to_row, to_col), device_id_type=MESH
            )
        )
    pl.semaphore_wait(barrier, sum(cond.astype(jnp.int32) for cond, _, _ in neighbours))

    def go_up(half, chunk, source, cond):
        send(cond & (line < lines - 1), source, slot(half, chunk), up_sem.at[half, chunk],
             row_sem.at[half, chunk], row, col + 2)

    def go_down(half, chunk, source, cond):
        send(cond & (line > 0), source, slot(half, chunk), down_sem.at[half, chunk],
             row_sem.at[half, chunk], row, col - 2)

    def go_side(half, chunk, source, cond):
        send(cond, source, slot(half, chunk), side_sem.at[half, chunk],
             row_sem.at[half, chunk], row, line * 2 + 1 - side)

    def spread_head(chunk, source, cond):
        cond = cond & (row % 2 == 0)
        target = piece(head_ref, chunk)
        send(cond, source, target, head_mate.at[chunk], head_sem.at[chunk], mate, col)
        send(cond & (row < row_count - 2), source, target, head_up.at[chunk], head_sem.at[chunk], row + 2, col)

    def spread_column(chunk, source, cond):
        cond = cond & (row % 2 == owner % 2)
        target = piece(column_ref, chunk)
        send(cond & (row >= owner) & (row < row_count - 2), source, target, col_up.at[chunk],
             col_sem.at[chunk], row + 2, col)
        send(cond & (row <= owner) & (row > 1), source, target, col_down.at[chunk],
             col_sem.at[chunk], row - 2, col)
        send(cond, source, target, col_mate.at[chunk], col_sem.at[chunk], mate, col)

    def pass_on(half, chunk, source, cond):
        if half == 0:
            spread_head(chunk, source, cond & (row == 0))
        spread_column(chunk, source, cond & (row == owner) & (part == half))

    always = row >= 0

    def own_sends(half):
        own = own_ref.at[half]
        go_side(half, col, own, always)
        go_up(half, col, own, always)
        go_down(half, col, own, always)
        pass_on(half, col, own, always)

    for half in range(halves):
        own_sends(half)
    for half in range(halves):
        rows_ref[half, pl.ds(pl.multiple_of(col * width, 8), width), :] = own_ref[half]

    order = [(0, line, always)]
    for away in range(1, lines):
        order.append((away, jnp.maximum(line - away, 0), line >= away))
        order.append((-away, jnp.minimum(line + away, lines - 1), line + away < lines))

    def row_event(half, away, at, cond):
        chunk = at * 2 + side
        if away != 0:
            arrived(cond, slot(half, chunk), row_sem.at[half, chunk])
            (go_up if away > 0 else go_down)(half, chunk, slot(half, chunk), cond)
            go_side(half, chunk, slot(half, chunk), cond)
            pass_on(half, chunk, slot(half, chunk), cond)
        chunk = at * 2 + 1 - side
        arrived(cond, slot(half, chunk), row_sem.at[half, chunk])
        pass_on(half, chunk, slot(half, chunk), cond)

    def head_event(at, cond):
        for chunk in (at * 2 + side, at * 2 + 1 - side):
            taken = cond & (row > 0)
            arrived(taken, piece(head_ref, chunk), head_sem.at[chunk])
            spread_head(chunk, piece(head_ref, chunk), taken)

    def col_event(at, cond):
        for chunk in (at * 2 + side, at * 2 + 1 - side):
            taken = cond & (row != owner)
            arrived(taken, piece(column_ref, chunk), col_sem.at[chunk])
            spread_column(chunk, piece(column_ref, chunk), taken)

    for away, at, cond in order:
        row_event(0, away, at, cond)
    rest = [
        functools.partial(row_event, half, away, at, cond)
        for half in range(1, halves)
        for away, at, cond in order
    ]
    heads = [functools.partial(head_event, at, cond) for _, at, cond in order]
    columns = [functools.partial(col_event, at, cond) for _, at, cond in order]

    def among(events, turns):
        def beside(turn):
            for number in range(turns):

                @pl.when(turn == number)
                def _(number=number):
                    for event in events[
                        len(events) * number // turns : len(events) * (number + 1) // turns
                    ]:
                        event()

        return beside

    depth = head_ref.shape[0]
    step = 2 * LANES if depth % (2 * LANES) == 0 else LANES
    col_start = col * centers
    first_row = row * halves * centers

    def send_inverse(cond):
        cond = cond & (row % 2 == 0)
        send(cond & (row < row_count - 2), inverse, inverse, inverse_sem.at[0], inverse_sem.at[2],
             row + 2, col)
        send(cond, inverse, inverse, inverse_sem.at[1], inverse_sem.at[2], mate, col)

    @pl.when(row == 0)
    def _():
        head_ref[...] = rows_ref[0]
        gauss_into(corner, head_ref, head_ref, 0, FINE, step)
        slots = centers // LANES
        late = [lambda: None] * (len(rest) // (slots - 1))
        factor_into(corner, chol, inverse, work, block, done, among(late + rest, slots))
        send_inverse(always)

    @pl.when(row > 0)
    def _():
        for number in range(max(len(rest), len(heads))):
            for event in rest[number : number + 1] + heads[number : number + 1]:
                event()
        gauss_into(side_tiles.at[0], rows_ref.at[0], head_ref, first_row, PLAIN, step,
                   among(columns, depth // step))

    @pl.when(row == 0)
    def _():
        if halves == 1:
            for event in columns:
                event()
        else:
            gauss_into(side_tiles.at[1], rows_ref.at[1], head_ref, first_row + centers, PLAIN, step,
                       among(columns, depth // step))

    @pl.when(row == owner)
    def _():
        column_ref[...] = rows_ref[part]

    def side_of(half, carry):
        gauss_into(side_tiles.at[half], rows_ref.at[half], head_ref, first_row + half * centers, PLAIN, step)
        return carry

    def tile_of(half, carry):
        here = pl.ds(pl.multiple_of(half * centers, centers), centers)
        gauss_into(trail_ref.at[here, :], rows_ref.at[half], column_ref,
                   first_row + half * centers - col_start, PLAIN, step)
        return carry

    lax.fori_loop(jnp.where(row == 0, 2, 1), halves, side_of, 0)
    lax.fori_loop(0, halves, tile_of, 0)
    gauss_into(far, column_ref, head_ref, col_start, PLAIN, step)

    arrived(row > 0, inverse, inverse_sem.at[2])
    send_inverse(row > 0)
    far[...] = jnp.where(col == 0, 0.0, product(far[...], inverse[...], 1, FINE))

    def finish(half, carry):
        here = pl.ds(pl.multiple_of(half * centers, centers), centers)
        solved = product(side_tiles[half], inverse[...], 1, FINE)
        panel_ref[here, :] = solved
        trail_ref[here, :] -= product(solved, far[...], 1, PLAIN)
        return carry

    lax.fori_loop(jnp.where(row == 0, 1, 0), halves, finish, 0)

    @pl.when(row == 0)
    def _():
        panel_ref[pl.ds(0, centers), :] = chol[...]

    def gone(cond, source, send_sem):
        pl.when(cond)(lambda: copy_of(source, source, send_sem, send_sem, row, col).wait_send())

    gone((row % 2 == 0) & (row < row_count - 2), inverse, inverse_sem.at[0])
    gone(row % 2 == 0, inverse, inverse_sem.at[1])
    for away, at, cond in order:
        chunk = at * 2 + side
        for half in range(halves):
            gone(cond & (line < lines - 1) & (at <= line), slot(half, chunk), up_sem.at[half, chunk])
            gone(cond & (line > 0) & (at >= line), slot(half, chunk), down_sem.at[half, chunk])
            gone(cond, slot(half, chunk), side_sem.at[half, chunk])
        for chunk in (at * 2 + side, at * 2 + 1 - side):
            head = piece(head_ref, chunk)
            gone(cond & (row % 2 == 0) & (row < row_count - 2), head, head_up.at[chunk])
            gone(cond & (row % 2 == 0), head, head_mate.at[chunk])
            ours = cond & (row % 2 == owner % 2)
            column = piece(column_ref, chunk)
            gone(ours & (row >= owner) & (row < row_count - 2), column, col_up.at[chunk])
            gone(ours & (row <= owner) & (row > 1), column, col_down.at[chunk])
            gone(ours, column, col_mate.at[chunk])


def factor_panel(turned, row_count, col_count):
    halves, width, centers = turned.shape
    depth = width * col_count
    dma = pltpu.SemaphoreType.DMA
    square = pltpu.VMEM((centers, centers), jnp.float32)
    return pl.pallas_call(
        functools.partial(panel_kernel, row_count, col_count),
        out_shape=[jax.ShapeDtypeStruct((halves * centers, centers), jnp.float32)] * 2,
        in_specs=[pl.BlockSpec(memory_space=pltpu.VMEM)],
        out_specs=[pl.BlockSpec(memory_space=pltpu.VMEM)] * 2,
        scratch_shapes=[
            pltpu.VMEM((halves, depth, centers), jnp.float32),
            pltpu.VMEM((depth, centers), jnp.float32),
            pltpu.VMEM((depth, centers), jnp.float32),
            square,
            square,
            square,
            square,
            pltpu.VMEM((halves, centers, centers), jnp.float32),
            pltpu.VMEM((centers, 2 * centers), jnp.float32),
            pltpu.VMEM((LANES, 2 * LANES), jnp.float32),
            pltpu.VMEM((LANES, 2 * LANES), jnp.float32),
            dma((3,)),
            dma((halves, col_count)),
            dma((col_count,)),
            dma((col_count,)),
            dma((halves, col_count)),
            dma((halves, col_count)),
            dma((halves, col_count)),
            dma((col_count,)),
            dma((col_count,)),
            dma((col_count,)),
            dma((col_count,)),
            dma((col_count,)),
        ],
        compiler_params=pltpu.CompilerParams(
            collective_id=0, has_side_effects=True, vmem_limit_bytes=56 * 1024 * 1024
        ),
        name="panel",
    )(turned)


def on_device(features):
    row_count = lax.axis_size("row")
    col_count = lax.axis_size("col")
    row_height, width = features.shape
    halves = col_count // row_count
    turned = features.reshape(halves, row_height // halves, width).transpose(0, 2, 1)
    return tuple(factor_panel(turned, row_count, col_count))


def solution(mesh):
    return jax.shard_map(
        on_device,
        mesh=mesh,
        in_specs=(P("row", "col"),),
        out_specs=(P("row", None), P("row", "col")),
        check_vma=False,
    )
```
